256 devices in a mesh: tm: 16 (over y, x_lo, core), space: 16 (over z, x_hi).
Axes of the slice: x: 4 (x_hi: 2, x_lo: 2; x = x_hi * 2 + x_lo), y: 4, z: 8, core: 2. Of those that a mesh axis runs over, the one named last changes fastest.
Arguments:
- video: bfloat16 [256, 64, 2048], P('space', 'tm'), may hold values from -120 to 120
- frame_ids: int32 [64], P('tm'), may hold values from 0 to 63, as said below
- gains: float32 [3, 2048], replicated, may hold values from 0.1 to 1.9
- spatial_qkv: bfloat16 [3, 2048, 2048], P(None, None, 'space'), may hold values from -2 to 2
- spatial_out: bfloat16 [2048, 2048], P('space'), may hold values from -0.75 to 0.75
- temporal_qkv: bfloat16 [3, 2048, 2048], P(None, None, 'space'), may hold values from -2 to 2
- temporal_out: bfloat16 [2048, 2048], P('space'), may hold values from -0.125 to 0.125
- mlp_in: bfloat16 [2048, 8192], P(None, 'space'), may hold values from -0.125 to 0.125
- mlp_out: bfloat16 [8192, 2048], P('space'), may hold values from -0.0625 to 0.0625
Outputs:
- block_out: bfloat16 [256, 64, 2048], P('space', 'tm')
The draws below stay inside these ranges and needn't reach their ends.
Inputs may be any that keep to these rules, and one draw needn't show every extreme that they name: `frame_ids`: a permutation of 0 to 63 in which frame slots 2j and 2j + 1 hold frames k and 63 - k for some k.
All inputs are finite; a program needn't handle non-finite values.
Results may differ from the reference program's by a relative error of at most 0.02.
Values may be sent and summed in bfloat16 or wider, within the bound.
No kernel may reach another device: no remote copies, remote signals or barrier semaphores. Data moves between devices by JAX's collectives and lax.ppermute only.
A program may use at most 128 MiB of HBM per device.

```python
import math
import jax
import jax.numpy as jnp
from jax import lax

D = 2048
HEADS = 16
FF = 8192
HEAD_DIM = 128
P_SIZE = 256
F = 64
N_SPACE = 16


def drawn_weights(key, constant):
    key = jax.random.fold_in(key, constant)
    key_weight = jax.random.fold_in(key, 0)
    weight = jnp.clip(jax.random.normal(key_weight, (3, D, D), jnp.float32), -6.0, 6.0) / math.sqrt(D)
    return weight.astype(jnp.bfloat16)


def draw_video(key, part):
    key = jax.random.fold_in(key, 3)
    key_noise = jax.random.fold_in(key, 0)
    noise = jnp.clip(jax.random.normal(key_noise, (P_SIZE, F, D), jnp.float32), -6.0, 6.0)
    return noise.astype(jnp.bfloat16)


def draw_spatial_qkv(key, part):
    return drawn_weights(key, 5)


def draw_temporal_qkv(key, part):
    return drawn_weights(key, 7)


def draw_frame_ids(key, part):
    key = jax.random.fold_in(key, 11)
    key_order, key_flip = jax.random.split(key)
    pairs = F // 2
    order = jax.random.permutation(key_order, pairs).astype(jnp.int32)
    flip = jax.random.randint(key_flip, (pairs,), 0, 2).astype(jnp.int32)
    leading = jnp.where(flip == 1, F - 1 - order, order)
    trailing = F - 1 - leading
    return jnp.stack([leading, trailing], axis=1).reshape(F).astype(jnp.int32)


def strengthened(drawn, key, source, target, shards_of, factor):
    owner, partner = [(jnp.arange(drawn.shape[position]) // (drawn.shape[position] // shards_of)).reshape([-1 if axis == position else 1 for axis in range(drawn.ndim)]) for position in (source, target)]
    chosen = jax.random.permutation(key, shards_of)[partner]
    strong = (owner == chosen) | (owner == (partner + shards_of // 2) % shards_of)
    return jnp.where(strong, factor * drawn, drawn)


def shard_levels(key, extent, cuts, smallest, high):
    factor_of, own = 1.0, jax.random.fold_in(key, 6)
    for axis_at, blocks in cuts:
        steps = jnp.exp(jax.random.uniform(jax.random.fold_in(own, axis_at), (blocks,), jnp.float32, smallest / len(cuts), high / len(cuts)))
        factor_of = factor_of * jnp.repeat(steps, extent[axis_at] // blocks).reshape([-1 if axis == axis_at else 1 for axis in range(len(extent))])
    return factor_of


def gaussian(rng, dims, deviation, bound, cuts=(), held_as=jnp.bfloat16):
    values = deviation * jax.random.normal(rng, dims, jnp.float32)
    if cuts:
        values = values * shard_levels(rng, dims, cuts, -0.22, 0.18)
    return jnp.clip(values, -bound, bound).astype(held_as)


def bell_draw_with(rng, shape, deviation, limit, pieces, heavy, kind=jnp.bfloat16):
    values = deviation * jax.random.normal(rng, shape, jnp.float32)
    if pieces:
        values = values * shard_levels(rng, shape, pieces, -0.22, 0.18)
    return jnp.clip(strengthened(values, jax.random.fold_in(rng, 3), *heavy), -limit, limit).astype(kind)


def setup_inputs(seed: int = 0) -> dict:
    key_list = jax.random.split(jax.random.key(seed), 10)
    video = draw_video(jax.random.fold_in(key_list[9], 71), 0)
    frame_ids = draw_frame_ids(jax.random.fold_in(key_list[9], 71), 0)
    gains = jnp.clip(1.0 + 0.18 * jax.random.normal(key_list[2], (3, D), jnp.float32), 0.1, 1.9)
    spatial_qkv = draw_spatial_qkv(jax.random.fold_in(key_list[9], 71), 0)
    spatial_out = bell_draw_with(key_list[4], (D, D), HEAD_DIM ** -0.5, 0.75, ((0, 16),), (0, 1, 16, 2.0))
    temporal_qkv = draw_temporal_qkv(jax.random.fold_in(key_list[9], 71), 0)
    temporal_out = gaussian(key_list[6], (D, D), D ** -0.5, 0.125, ((0, 16),))
    mlp_in = gaussian(key_list[7], (D, FF), D ** -0.5, 0.125, ((1, 16),))
    mlp_out = gaussian(key_list[8], (FF, D), FF ** -0.5, 0.0625, ((0, 16),))
    return dict(video=video, frame_ids=frame_ids, gains=gains, spatial_qkv=spatial_qkv, spatial_out=spatial_out, temporal_qkv=temporal_qkv, temporal_out=temporal_out, mlp_in=mlp_in, mlp_out=mlp_out)


def normed(value, gain):
    meansq = lax.optimization_barrier(jnp.mean(value * value, axis=-1, keepdims=True))
    return value * lax.rsqrt(meansq + 1e-06) * gain

def rounded(value):
    return lax.optimization_barrier(value.astype(jnp.bfloat16)).astype(jnp.float32)

def blockwise(left, weight):
    width = left.shape[1] // N_SPACE
    start_acc = jnp.zeros((left.shape[0], weight.shape[1]), jnp.float32)

    def step(accum, group):
        begin = (group * width).astype(jnp.int32)
        lpart = lax.dynamic_slice_in_dim(left, begin, width, 1)
        wpart = lax.dynamic_slice_in_dim(weight, begin, width, 0)
        partial_sum = jnp.dot(lpart, wpart, preferred_element_type=jnp.float32)
        return (accum + rounded(partial_sum), None)
    accum, _ = lax.scan(step, start_acc, jnp.arange(N_SPACE, dtype=jnp.int32))
    return accum

def reference(video, frame_ids, gains, spatial_qkv, spatial_out, temporal_qkv, temporal_out, mlp_in, mlp_out):
    total = P_SIZE * F
    scale = 1.0 / math.sqrt(HEAD_DIM)
    state = video.astype(jnp.float32)
    first = normed(state, gains[0]).astype(jnp.bfloat16).reshape(total, D)

    def heads(source, weight, index):
        proj = jnp.dot(source, weight[index], preferred_element_type=jnp.float32)
        return rounded(proj).reshape(P_SIZE, F, HEADS, HEAD_DIM)
    query = heads(first, spatial_qkv, 0)
    keys = heads(first, spatial_qkv, 1)
    values = heads(first, spatial_qkv, 2)
    scores = jnp.einsum('pfhe,qfhe->fhpq', query, keys) * scale
    weights = rounded(jax.nn.softmax(scores, axis=-1))
    spatial = jnp.einsum('fhpq,qfhe->pfhe', weights, values).astype(jnp.bfloat16).reshape(total, D)
    second_state = state + blockwise(spatial, spatial_out).reshape(P_SIZE, F, D)
    second = normed(second_state, gains[1]).astype(jnp.bfloat16).reshape(total, D)
    tquery = heads(second, temporal_qkv, 0)
    tkeys = heads(second, temporal_qkv, 1)
    tvalues = heads(second, temporal_qkv, 2)
    tscores = jnp.einsum('pfhe,pghe->phfg', tquery, tkeys) * scale
    visible = frame_ids[None, :] <= frame_ids[:, None]
    tscores = jnp.where(visible[None, None], tscores, -1e+30)
    tweights = jax.nn.softmax(tscores, axis=-1)
    temporal = jnp.einsum('phfg,pghe->pfhe', tweights, tvalues, precision=lax.Precision.HIGHEST)
    temporal = temporal.astype(jnp.bfloat16).reshape(total, D)
    third_state = second_state + blockwise(temporal, temporal_out).reshape(P_SIZE, F, D)
    third = normed(third_state, gains[2]).astype(jnp.bfloat16).reshape(total, D)
    hidden = jax.nn.gelu(jnp.dot(third, mlp_in, preferred_element_type=jnp.float32), approximate=True).astype(jnp.bfloat16)
    result = third_state + blockwise(hidden, mlp_out).reshape(P_SIZE, F, D)
    return result.astype(jnp.bfloat16)
```

```python
import math

import jax
import jax.numpy as jnp
from jax import lax
from jax.experimental import pallas as pl
from jax.experimental.pallas import tpu as pltpu
from jax.sharding import Mesh, PartitionSpec as P

HEAD_DIM = 128
SCALE = 1.0 / math.sqrt(HEAD_DIM)
F32 = jnp.float32
BF16 = jnp.bfloat16
TM = ("y", "xl", "c")
PEERS = ("y", "xl", "c", "xh")
SWAP = [(0, 1), (1, 0)]
MIB = 1 << 20


def normed(value, gain):
    meansq = jnp.mean(value * value, axis=-1, keepdims=True)
    return value * lax.rsqrt(meansq + 1e-06) * gain


def dot(a, b):
    return jnp.dot(a, b, preferred_element_type=F32)


def dot_t(a, b):
    return lax.dot_general(a, b, (((1,), (1,)), ((), ())), preferred_element_type=F32)


def ring_gather(block, tied=None):
    size = 8
    right = [(i, (i + 1) % size) for i in range(size)]
    left = [(i, (i - 1) % size) for i in range(size)]
    z = lax.axis_index("z")
    rows = block.shape[0]
    out = jnp.zeros((size,) + block.shape, block.dtype)
    put = lambda out, part, owner, row: lax.dynamic_update_slice(
        out, part[None], (lax.rem(owner + 2 * size, size), row, 0)
    )
    out = put(out, block, z, 0)
    fwd = bwd = block
    for step in range(1, 4):
        fwd = lax.ppermute(fwd, "z", right)
        bwd = lax.ppermute(bwd, "z", left)
        out = put(out, fwd, z - step, 0)
        out = put(out, bwd, z + step, 0)
    if tied is not None:
        fwd, bwd, tied = lax.optimization_barrier((fwd, bwd, tied))
    half = rows // 2
    fwd = lax.ppermute(fwd[:half], "z", right)
    bwd = lax.ppermute(bwd[half:], "z", left)
    out = put(out, fwd, z - 4, 0)
    out = put(out, bwd, z + 4, half)
    return out, tied


def spatial_kernel(first_ref, h_ref, own_ref, other_ref, out_ref):
    rows = h_ref.shape[0]
    frame_q = (lax.broadcasted_iota(jnp.int32, (rows, rows), 0) // 8) % 2
    frame_k = (lax.broadcasted_iota(jnp.int32, (rows, rows), 1) // 8) % 2
    same = frame_q == frame_k
    hidden = h_ref[...]

    def head(w_ref):
        query = dot(hidden, w_ref[0]).astype(BF16)
        keys = dot(hidden, w_ref[1]).astype(BF16)
        values = dot(hidden, w_ref[2]).astype(BF16)
        scores = jnp.where(same, dot_t(query, keys) * SCALE, -1e30)
        top = jnp.max(scores, axis=-1, keepdims=True)
        probs = jnp.exp(scores - top)
        total = jnp.sum(probs, axis=-1, keepdims=True)
        weights = (probs / total).astype(BF16)
        return dot(weights, values).astype(BF16)

    mine, other = head(own_ref), head(other_ref)
    swap = first_ref[0] == 0
    out_ref[:, :HEAD_DIM] = jnp.where(swap, mine, other)
    out_ref[:, HEAD_DIM:] = jnp.where(swap, other, mine)


def spatial(position, hidden, own, other):
    rows = hidden.shape[0]
    vmem = pl.BlockSpec(memory_space=pltpu.VMEM)
    return pl.pallas_call(
        spatial_kernel,
        out_shape=jax.ShapeDtypeStruct((rows, 2 * HEAD_DIM), BF16),
        in_specs=[pl.BlockSpec(memory_space=pltpu.SMEM), vmem, vmem, vmem],
        out_specs=vmem,
        compiler_params=pltpu.CompilerParams(vmem_limit_bytes=48 * MIB),
        name="spatial",
    )(position, hidden, own, other)


def out_kernel(part_ref, w_ref, state_ref, gain_ref, x_ref, h_ref):
    step = pl.program_id(0)
    width = w_ref.shape[2]
    depth = part_ref.shape[2]
    total = jnp.zeros((part_ref.shape[1], width), F32)
    for z in range(part_ref.shape[0]):
        total += dot(part_ref[z], w_ref[0, z * depth : (z + 1) * depth])
    columns = pl.ds(pl.multiple_of(step * width, width), width)
    x_ref[:, columns] = state_ref[:, columns].astype(F32) + total

    @pl.when(step == pl.num_programs(0) - 1)
    def _():
        h_ref[...] = normed(x_ref[...], gain_ref[...]).astype(BF16)


def out_project(parts, weight, state, gain):
    blocks, rows, depth = parts.shape
    columns, inputs, width = weight.shape
    model = columns * width
    return pl.pallas_call(
        out_kernel,
        grid=(columns,),
        out_shape=(
            jax.ShapeDtypeStruct((rows, model), F32),
            jax.ShapeDtypeStruct((rows, model), BF16),
        ),
        in_specs=[
            pl.BlockSpec((blocks, rows, depth), lambda c: (0, 0, 0)),
            pl.BlockSpec((1, inputs, width), lambda c: (c, 0, 0)),
            pl.BlockSpec((rows, model), lambda c: (0, 0)),
            pl.BlockSpec((1, model), lambda c: (0, 0)),
        ],
        out_specs=(
            pl.BlockSpec((rows, model), lambda c: (0, 0)),
            pl.BlockSpec((rows, model), lambda c: (0, 0)),
        ),
        compiler_params=pltpu.CompilerParams(vmem_limit_bytes=32 * MIB),
        name="out_project",
    )(parts, weight, state, gain)


def temporal_kernel(qkv_ref, seen_ref, out_ref):
    seen = seen_ref[...] > 0
    for head in range(2):
        pick = lambda kind: qkv_ref[
            :, (2 * kind + head) * HEAD_DIM : (2 * kind + head + 1) * HEAD_DIM
        ]
        query, keys, values = pick(0), pick(1), pick(2)
        scores = jnp.where(seen, dot_t(query, keys) * SCALE, -1e30)
        top = jnp.max(scores, axis=-1, keepdims=True)
        probs = jnp.exp(scores - top)
        total = jnp.sum(probs, axis=-1, keepdims=True)
        coarse = probs.astype(BF16)
        fine = (probs - coarse.astype(F32)).astype(BF16)
        result = (dot(coarse, values) + dot(fine, values)) / total
        out_ref[:, head * HEAD_DIM : (head + 1) * HEAD_DIM] = result.astype(BF16)


def temporal(qkv, seen):
    vmem = pl.BlockSpec(memory_space=pltpu.VMEM)
    return pl.pallas_call(
        temporal_kernel,
        out_shape=jax.ShapeDtypeStruct((qkv.shape[0], 2 * HEAD_DIM), BF16),
        in_specs=[vmem, vmem],
        out_specs=vmem,
        compiler_params=pltpu.CompilerParams(vmem_limit_bytes=48 * MIB),
        name="temporal",
    )(qkv, seen)


def project_kernel(first_ref, h_ref, own_ref, other_ref, out_ref):
    swap = first_ref[0] == 0
    hidden = h_ref[...]
    for kind in range(3):
        mine = dot(hidden, own_ref[kind]).astype(BF16)
        other = dot(hidden, other_ref[kind]).astype(BF16)
        start = 2 * kind * HEAD_DIM
        out_ref[:, start : start + HEAD_DIM] = jnp.where(swap, mine, other)
        out_ref[:, start + HEAD_DIM : start + 2 * HEAD_DIM] = jnp.where(swap, other, mine)


def project(position, hidden, own, other):
    vmem = pl.BlockSpec(memory_space=pltpu.VMEM)
    return pl.pallas_call(
        project_kernel,
        out_shape=jax.ShapeDtypeStruct((hidden.shape[0], 6 * HEAD_DIM), BF16),
        in_specs=[pl.BlockSpec(memory_space=pltpu.SMEM), vmem, vmem, vmem],
        out_specs=vmem,
        compiler_params=pltpu.CompilerParams(vmem_limit_bytes=32 * MIB),
        name="project",
    )(position, hidden, own, other)


def mlp_kernel(h_ref, in_ref, in2_ref, out_ref, out2_ref, o_ref):
    @pl.loop(0, h_ref.shape[0] // 256)
    def _(tile):
        rows = pl.ds(pl.multiple_of(tile * 256, 256), 256)
        hidden = h_ref[rows]
        total = None
        for w_in, w_out in ((in_ref, out_ref), (in2_ref, out2_ref)):
            inner = jax.nn.gelu(dot(hidden, w_in[...]), approximate=True).astype(BF16)
            term = dot(inner, w_out[...])
            total = term if total is None else total + term
        o_ref[rows] = total.astype(BF16)


def mlp(hidden, w_in, in_other, w_out, out_other):
    vmem = pl.BlockSpec(memory_space=pltpu.VMEM)
    return pl.pallas_call(
        mlp_kernel,
        out_shape=jax.ShapeDtypeStruct(hidden.shape, BF16),
        in_specs=[vmem] * 5,
        out_specs=vmem,
        compiler_params=pltpu.CompilerParams(vmem_limit_bytes=48 * MIB),
        name="mlp",
    )(hidden, w_in, in_other, w_out, out_other)


def body(
    video, frame_ids, gains, spatial_qkv, spatial_out, temporal_qkv, temporal_out, mlp_in, mlp_out
):
    xh = lax.axis_index("xh")
    model = video.shape[-1]
    first = xh == 0
    place = xh.astype(jnp.int32).reshape(1)

    def after(value, earlier):
        return lax.optimization_barrier((value, earlier))[0]

    def piece(weight):
        block = lax.axis_index("y") * 2 + lax.axis_index("c")
        width = model // 8
        own = lax.dynamic_slice_in_dim(weight, block * width, width, 1)
        other = lax.ppermute(own, "xh", SWAP)
        return jnp.concatenate(
            [jnp.where(first, own, other), jnp.where(first, other, own)], axis=0
        )

    def along_z(part):
        return lax.all_gather(part, "z", axis=0, tiled=True)

    def blocks(part):
        return lax.all_gather(part, ("y", "c"), axis=0)

    grouped = jnp.transpose(video.reshape(2, 8, 4, model), (0, 2, 1, 3))
    keep = lax.dynamic_slice_in_dim(grouped, 2 * xh, 2, 1)
    give = lax.dynamic_slice_in_dim(grouped, 2 * (1 - xh), 2, 1)
    got = lax.ppermute(give, "xh", SWAP)
    state = jnp.concatenate(
        [jnp.where(first, keep, got), jnp.where(first, got, keep)], axis=0
    ).reshape(64, model)

    hidden = normed(state.astype(F32), gains[0]).astype(BF16)
    spatial_part = along_z(piece(spatial_out))
    temporal_part = piece(after(temporal_out, spatial_part))
    spatial_other = lax.ppermute(after(spatial_qkv, got), "xh", SWAP)
    hidden, spatial_part = ring_gather(hidden, spatial_part)
    spatial_whole = blocks(spatial_part)
    temporal_other = lax.ppermute(after(temporal_qkv, spatial_other), "xh", SWAP)
    heads = spatial(place, hidden.reshape(512, model), spatial_qkv, spatial_other)
    parts = lax.all_to_all(heads.reshape(8, 64, 256), "z", 0, 0, tiled=True)
    second, hidden = out_project(parts, spatial_whole, state, gains[1:2])

    stamps = lax.dynamic_slice_in_dim(frame_ids, 2 * xh, 2, 0).astype(F32)
    stamps = jnp.broadcast_to(stamps[:, None, None], (2, 8, 128)).reshape(16, 128)
    stamps = lax.all_gather(after(stamps, hidden), PEERS, axis=0, tiled=True)
    temporal_part = along_z(after(temporal_part, hidden))
    hidden, (temporal_part, stamps) = ring_gather(hidden, (temporal_part, stamps))
    temporal_whole = blocks(temporal_part)
    stamps = stamps[:, :1]
    count = stamps.shape[0]
    token = jnp.arange(count, dtype=jnp.int32) % 8
    seen = (stamps.reshape(1, count) <= stamps) & (token[None, :] == token[:, None])

    packed = project(place, hidden.reshape(512, model), temporal_qkv, temporal_other)
    in_other = lax.ppermute(after(mlp_in, packed), "xh", SWAP)
    packed = lax.all_to_all(packed.reshape(32, 16, 768), PEERS, 0, 0, tiled=True)
    heads = temporal(packed.reshape(512, 768), seen.astype(F32))
    heads = lax.all_to_all(heads.reshape(32, 16, 256), PEERS, 0, 0, tiled=True)
    out_other = lax.ppermute(after(mlp_out, heads), "xh", SWAP)
    parts = lax.all_to_all(heads.reshape(8, 64, 256), "z", 0, 0, tiled=True)
    third, hidden = out_project(parts, temporal_whole, second, gains[2:3])

    hidden, _ = ring_gather(hidden)
    partial = mlp(hidden.reshape(512, model), mlp_in, in_other, mlp_out, out_other)
    parts = lax.all_to_all(partial.reshape(8, 64, model), "z", 0, 0, tiled=True)
    result = (third + jnp.sum(parts.astype(F32), axis=0)).astype(BF16)

    result = result.reshape(2, 2, 2, 8, model)
    keep = lax.dynamic_index_in_dim(result, xh, 0, keepdims=False)
    give = lax.dynamic_index_in_dim(result, 1 - xh, 0, keepdims=False)
    got = lax.ppermute(give, "xh", SWAP)
    result = jnp.concatenate([jnp.where(first, keep, got), jnp.where(first, got, keep)], axis=1)
    return jnp.transpose(result, (0, 2, 1, 3)).reshape(16, 4, model)


def solution(mesh):
    fine = Mesh(mesh.devices.reshape(4, 2, 2, 8, 2), ("y", "xl", "c", "z", "xh"))
    space = ("z", "xh")
    return jax.shard_map(
        body,
        mesh=fine,
        in_specs=(
            P(space, TM, None),
            P(TM),
            P(),
            P(None, None, space),
            P(space, None),
            P(None, None, space),
            P(space, None),
            P(None, space),
            P(space, None),
        ),
        out_specs=P(space, TM, None),
        check_vma=False,
    )
```

```python
import math

import jax
import jax.numpy as jnp
from jax import lax
from jax.experimental import pallas as pl
from jax.experimental.pallas import tpu as pltpu
from jax.sharding import Mesh, PartitionSpec as P

HEAD_DIM = 128
SCALE = 1.0 / math.sqrt(HEAD_DIM)
F32 = jnp.float32
BF16 = jnp.bfloat16
TM = ("y", "xl", "c")
Z = ("zp", "zl")
SPACE = ("zp", "zl", "xh")
PEERS = ("y", "xl", "c", "xh")
SWAP = [(0, 1), (1, 0)]
MIB = 1 << 20


def normed(value, gain):
    meansq = jnp.mean(value * value, axis=-1, keepdims=True)
    return value * lax.rsqrt(meansq + 1e-06) * gain


def dot(a, b):
    return jnp.dot(a, b, preferred_element_type=F32)


def dot_t(a, b):
    return lax.dot_general(a, b, (((1,), (1,)), ((), ())), preferred_element_type=F32)


def tie(*values):
    return lax.optimization_barrier(values)


def ring(size):
    return [(i, (i + 1) % size) for i in range(size)], [(i, (i - 1) % size) for i in range(size)]


def x_swap(value):
    return lax.ppermute(value, "xh", SWAP)


class Beside:
    def __init__(self, values):
        self.values = list(values)
        self.results = []

    def start(self, moving):
        if len(self.results) < len(self.values):
            self.results.append(x_swap(tie(self.values[len(self.results)], moving)[0]))

    def end(self, *moving):
        if len(self.results) > 1:
            *moving, self.results[-2] = tie(*moving, self.results[-2])
        return moving


def ring_gather(block, axis, by_rows=True, values=()):
    size = lax.axis_size(axis)
    right, left = ring(size)
    here = lax.axis_index(axis)
    rows, columns = block.shape
    beside = Beside(values)
    out = jnp.zeros((size * rows, columns) if by_rows else (rows, size * columns), block.dtype)

    def put(out, part, owner, row):
        owner = lax.rem(owner + size, size)
        at = (owner * rows + row, 0) if by_rows else (row, owner * columns)
        return lax.dynamic_update_slice(out, part, at)

    out = put(out, block, here, 0)
    fwd = bwd = block
    for step in range(1, size // 2):
        beside.start(fwd)
        fwd = lax.ppermute(fwd, axis, right)
        bwd = lax.ppermute(bwd, axis, left)
        fwd, bwd = beside.end(fwd, bwd)
        out = put(out, fwd, here - step, 0)
        out = put(out, bwd, here + step, 0)
    half = rows // 2
    far = here - size // 2
    fwd = lax.ppermute(fwd[:half], axis, right)
    bwd = lax.ppermute(bwd[half:], axis, left)
    out = put(out, fwd, far, 0)
    return put(out, bwd, far, half), beside.results


def ring_scatter(partial, axis):
    size = lax.axis_size(axis)
    right, left = ring(size)
    here = lax.axis_index(axis)
    rows, half = partial.shape[0] // size, partial.shape[1] // 2

    def term(offset):
        return lax.dynamic_slice_in_dim(partial, lax.rem(here + offset + size, size) * rows, rows, 0)

    def add(a, b):
        return (a.astype(F32) + b.astype(F32)).astype(BF16)

    far = term(size // 2)
    fwd = lax.ppermute(far[:, :half], axis, right)
    bwd = lax.ppermute(far[:, half:], axis, left)
    for step in range(size // 2 - 1, 0, -1):
        ahead, behind = term(step), term(-step)
        if step == size // 2 - 1:
            fwd = jnp.concatenate([add(ahead[:, :half], fwd), ahead[:, half:]], axis=1)
            bwd = jnp.concatenate([behind[:, :half], add(behind[:, half:], bwd)], axis=1)
        else:
            fwd, bwd = add(ahead, fwd), add(behind, bwd)
        fwd = lax.ppermute(fwd, axis, right)
        bwd = lax.ppermute(bwd, axis, left)
    return term(0), fwd, bwd


def vmem_call(kernel, outs, name, limit, scratch=()):
    vmem = pl.BlockSpec(memory_space=pltpu.VMEM)

    def call(position, *args):
        return pl.pallas_call(
            kernel,
            out_shape=outs,
            in_specs=[pl.BlockSpec(memory_space=pltpu.SMEM)] + [vmem] * len(args),
            out_specs=jax.tree.map(lambda _: vmem, outs),
            scratch_shapes=scratch,
            compiler_params=pltpu.CompilerParams(vmem_limit_bytes=limit * MIB),
            name=name,
        )(position, *args)

    return call


def shape(rows, columns, dtype=BF16):
    return jax.ShapeDtypeStruct((rows, columns), dtype)


def attend(query, keys, values, seen):
    scores = jnp.where(seen, dot_t(query, keys) * SCALE, -1e30)
    probs = jnp.exp(scores - jnp.max(scores, axis=-1, keepdims=True))
    return probs, jnp.sum(probs, axis=-1, keepdims=True)


def spatial_kernel(place_ref, x_ref, gain_ref, own_ref, a_ref, b_ref, out_ref, h_ref):
    rows, model = x_ref.shape
    frame_q = (lax.broadcasted_iota(jnp.int32, (rows, rows), 0) // 8) % 2
    frame_k = (lax.broadcasted_iota(jnp.int32, (rows, rows), 1) // 8) % 2
    same = frame_q == frame_k
    core, position = place_ref[0], place_ref[1]
    half = model // 2
    first = pl.ds(pl.multiple_of(core * half, half), half)
    second = pl.ds(pl.multiple_of((1 - core) * half, half), half)

    @pl.loop(0, rows // 128)
    def _(tile):
        part = pl.ds(pl.multiple_of(tile * 128, 128), 128)
        h_ref[part] = normed(x_ref[part].astype(F32), gain_ref[...]).astype(BF16)

    def head(query, keys, values):
        probs, total = attend(query.astype(BF16), keys.astype(BF16), values.astype(BF16), same)
        return dot((probs / total).astype(BF16), values.astype(BF16)).astype(BF16)

    def split(kind):
        return dot(h_ref[:, first], a_ref[kind]) + dot(h_ref[:, second], b_ref[kind])

    hidden = h_ref[...]
    mine = head(*(dot(hidden, own_ref[kind]) for kind in range(3)))
    other = head(*(split(kind) for kind in range(3)))
    out_ref[:, :HEAD_DIM] = jnp.where(position == 0, mine, other)
    out_ref[:, HEAD_DIM:] = jnp.where(position == 0, other, mine)


def project_kernel(place_ref, h_ref, own_ref, q0, q1, k0, k1, v0, v1, out_ref):
    rows, model = h_ref.shape
    core, position = place_ref[0], place_ref[1]
    half = model // 2
    first = pl.ds(pl.multiple_of(core * half, half), half)
    second = pl.ds(pl.multiple_of((1 - core) * half, half), half)
    hidden = h_ref[...]
    for kind, (a, b) in enumerate(((q0, q1), (k0, k1), (v0, v1))):
        mine = dot(hidden, own_ref[kind]).astype(BF16)
        other = (dot(h_ref[:, first], a[...]) + dot(h_ref[:, second], b[...])).astype(BF16)
        start = 2 * kind * HEAD_DIM
        out_ref[:, start : start + HEAD_DIM] = jnp.where(position == 0, mine, other)
        out_ref[:, start + HEAD_DIM : start + 2 * HEAD_DIM] = jnp.where(position == 0, other, mine)
    frame = (lax.broadcasted_iota(jnp.int32, (rows, HEAD_DIM), 0) // 8) % 2
    times = jnp.where(frame == 0, place_ref[2], place_ref[3])
    out_ref[:, 6 * HEAD_DIM :] = times.astype(F32).astype(BF16)


def temporal_kernel(_, qkv_ref, out_ref):
    rows = qkv_ref.shape[0]
    times = qkv_ref[:, 6 * HEAD_DIM :].astype(F32)
    token_q = lax.broadcasted_iota(jnp.int32, (rows, rows), 0) % 8
    token_k = lax.broadcasted_iota(jnp.int32, (rows, rows), 1) % 8
    seen = (jnp.transpose(times)[:1] <= times[:, :1]) & (token_q == token_k)
    for head in range(2):
        query, keys, values = (
            qkv_ref[:, (2 * kind + head) * HEAD_DIM : (2 * kind + head + 1) * HEAD_DIM]
            for kind in range(3)
        )
        probs, total = attend(query, keys, values, seen)
        coarse = probs.astype(BF16)
        fine = (probs - coarse.astype(F32)).astype(BF16)
        result = (dot(coarse, values) + dot(fine, values)) / total
        out_ref[:, head * HEAD_DIM : (head + 1) * HEAD_DIM] = result.astype(BF16)


def out_kernel(heads_ref, w_ref, w2_ref, state_ref, gain_ref, x_ref, h_ref, all_ref):
    step = pl.program_id(0)
    width, half = w_ref.shape[2], w_ref.shape[1]
    total = dot(heads_ref[:, :half], w_ref[0]) + dot(heads_ref[:, half:], w2_ref[0])
    total += state_ref[...].astype(F32)
    x_ref[...] = total
    all_ref[:, pl.ds(pl.multiple_of(step * width, width), width)] = total

    @pl.when(step == pl.num_programs(0) - 1)
    def _():
        @pl.loop(0, all_ref.shape[0] // 128)
        def _(tile):
            part = pl.ds(pl.multiple_of(tile * 128, 128), 128)
            h_ref[part] = normed(all_ref[part], gain_ref[...]).astype(BF16)


def out_project(heads, weight, state, gain):
    rows, inputs = heads.shape
    blocks, _, width = weight.shape
    model = blocks * width
    column = pl.BlockSpec((rows, width), lambda c: (0, c))
    return pl.pallas_call(
        out_kernel,
        grid=(blocks,),
        out_shape=(shape(rows, model, F32), shape(rows, model)),
        in_specs=[
            pl.BlockSpec((rows, inputs), lambda c: (0, 0)),
            pl.BlockSpec((1, inputs // 2, width), lambda c: (c, 0, 0)),
            pl.BlockSpec((1, inputs // 2, width), lambda c: (c, 1, 0)),
            column,
            pl.BlockSpec((1, model), lambda c: (0, 0)),
        ],
        out_specs=(column, pl.BlockSpec((rows, model), lambda c: (0, 0))),
        scratch_shapes=[pltpu.VMEM((rows, model), F32)],
        compiler_params=pltpu.CompilerParams(vmem_limit_bytes=56 * MIB),
        name="out_project",
    )(heads, weight, weight, state, gain)


def mlp_kernel(_, h_ref, in_ref, out_ref, *refs):
    *pieces, o_ref = refs
    ins, outs = (pieces[:3], pieces[5:8]), (pieces[3:5], pieces[8:])

    @pl.loop(0, h_ref.shape[0] // 256)
    def _(tile):
        rows = pl.ds(pl.multiple_of(tile * 256, 256), 256)

        def inner(weights):
            total, start = None, 0
            for w in weights:
                term = dot(h_ref[rows, start : start + w.shape[0]], w[...])
                total = term if total is None else total + term
                start += w.shape[0]
            return jax.nn.gelu(total, approximate=True).astype(BF16)

        units = jnp.concatenate([inner([in_ref]), inner(ins[0]), inner(ins[1])], axis=1)
        for block in range(o_ref.shape[1] // 256):
            columns = slice(block * 256, (block + 1) * 256)
            weight = [out_ref[:, columns]] + [w[:, columns] for w in (*outs[0], *outs[1])]
            o_ref[rows, columns] = dot(units, jnp.concatenate(weight, axis=0)).astype(BF16)


def body(
    video, frame_ids, gains, spatial_qkv, spatial_out, temporal_qkv, temporal_out, mlp_in, mlp_out
):
    xh, core = lax.axis_index("xh"), lax.axis_index("c")
    model = video.shape[-1]
    first = xh == 0
    times = lax.dynamic_slice_in_dim(frame_ids, 2 * xh, 2, 0)
    place = jnp.concatenate([jnp.stack([core, xh]).astype(jnp.int32), times])

    def cut(value, index, parts, axis):
        size = value.shape[axis] // parts
        return lax.dynamic_slice_in_dim(value, index * size, size, axis)

    def core_swap(value):
        return lax.ppermute(value, "c", SWAP)

    grouped = jnp.transpose(video.reshape(2, 8, 4, model), (0, 2, 1, 3))
    got = x_swap(cut(grouped, 1 - xh, 2, 1))
    keep = cut(grouped, xh, 2, 1)
    state = jnp.concatenate(
        [jnp.where(first, keep, got), jnp.where(first, got, keep)], axis=0
    ).reshape(64, model)
    def piece(weight):
        return cut(weight, lax.axis_index("y") * 2 + core, 8, 1)

    def paired(own, other):
        return jnp.concatenate([jnp.where(first, own, other), jnp.where(first, other, own)], axis=0)

    spatial_piece, temporal_piece = piece(spatial_out), piece(temporal_out)
    other = x_swap(jnp.concatenate([spatial_piece, temporal_piece], axis=1))
    state, other = tie(state, other)
    spatial_piece = paired(spatial_piece, other[:, :256])
    temporal_piece = paired(temporal_piece, other[:, 256:])
    spatial_piece = lax.all_gather(spatial_piece, Z, axis=0, tiled=True)

    temporal_half = cut(temporal_qkv, core, 2, 1)
    in_half, out_half = cut(mlp_in, core, 2, 1), cut(mlp_out, core, 2, 0)

    state, (other,) = ring_gather(state, Z, True, [cut(spatial_qkv, core, 2, 1)])
    state, spatial_piece, other = tie(state, spatial_piece, other)
    spatial_whole = lax.all_gather(spatial_piece, ("y", "c"), axis=0)
    in_a = x_swap(tie(in_half[:512], state)[0])
    heads = vmem_call(
        spatial_kernel, shape(512, 256), "spatial", 24, scratch=[pltpu.VMEM((512, model), BF16)]
    )(place, state, gains[:1], spatial_qkv, other, core_swap(other))
    heads, in_a = tie(heads, in_a)

    heads, others = ring_gather(heads, Z, False, [temporal_half[kind] for kind in range(3)])
    heads, *others = tie(heads, *others)
    pairs = [half for other in others for half in (other, core_swap(other))]
    in_b = x_swap(tie(in_half[512:1536], heads)[0])
    temporal_piece = lax.all_gather(tie(temporal_piece, spatial_whole)[0], Z, axis=0, tiled=True)
    second, hidden = out_project(heads, spatial_whole, state, gains[1:2])
    hidden, in_b = tie(hidden, in_b)
    packed = vmem_call(project_kernel, shape(512, 7 * HEAD_DIM), "project", 20)(
        place, hidden, temporal_qkv, *pairs
    )
    packed = lax.all_to_all(packed.reshape(32, 16, 7 * HEAD_DIM), PEERS, 0, 0, tiled=True)
    packed, temporal_piece = tie(packed, temporal_piece)
    temporal_whole = lax.all_gather(temporal_piece, ("y", "c"), axis=0)
    heads = vmem_call(temporal_kernel, shape(512, 2 * HEAD_DIM), "temporal", 20)(
        place, packed.reshape(512, 7 * HEAD_DIM)
    )
    heads = lax.all_to_all(heads.reshape(32, 16, 2 * HEAD_DIM), PEERS, 0, 0, tiled=True)
    heads, others = ring_gather(
        heads.reshape(512, 256), Z, False, [in_half[1536:], out_half[:128], out_half[128:]]
    )
    others = [in_a, in_b] + others
    third, hidden = out_project(heads, temporal_whole, second, gains[2:3])
    partial = vmem_call(mlp_kernel, shape(512, model), "mlp", 32)(
        place, hidden, mlp_in, mlp_out, *others, *(core_swap(other) for other in others)
    )
    own, fwd, bwd = ring_scatter(partial, Z)
    third = lax.dynamic_slice_in_dim(third, lax.axis_index(Z) * 64, 64, 0)
    result = third + (own.astype(F32) + fwd.astype(F32) + bwd.astype(F32))

    result = result.astype(BF16).reshape(2, 2, 2, 8, model)
    keep = lax.dynamic_index_in_dim(result, xh, 0, keepdims=False)
    got = x_swap(lax.dynamic_index_in_dim(result, 1 - xh, 0, keepdims=False))
    result = jnp.concatenate([jnp.where(first, keep, got), jnp.where(first, got, keep)], axis=1)
    return jnp.transpose(result, (0, 2, 1, 3)).reshape(16, 4, model)


def solution(mesh):
    fine = Mesh(mesh.devices.reshape(4, 2, 2, 4, 2, 2), TM + SPACE)
    return jax.shard_map(
        body,
        mesh=fine,
        in_specs=(
            P(SPACE, TM, None),
            P(TM),
            P(),
            P(None, None, SPACE),
            P(SPACE, None),
            P(None, None, SPACE),
            P(SPACE, None),
            P(None, SPACE),
            P(SPACE, None),
        ),
        out_specs=P(SPACE, TM, None),
        check_vma=False,
    )
```

```python
import math

import jax
import jax.numpy as jnp
from jax import lax
from jax.experimental import pallas as pl
from jax.experimental.pallas import tpu as pltpu
from jax.sharding import Mesh, PartitionSpec as P

HEAD_DIM = 128
SCALE = 1.0 / math.sqrt(HEAD_DIM)
F32 = jnp.float32
BF16 = jnp.bfloat16
TM = ("y", "xl", "c")
Z = ("zp", "zl")
SPACE = ("zp", "zl", "xh")
PEERS = ("y", "xl", "c", "xh")
SWAP = [(0, 1), (1, 0)]
MIB = 1 << 20


def normed(value, gain):
    meansq = jnp.mean(value * value, axis=-1, keepdims=True)
    return value * lax.rsqrt(meansq + 1e-06) * gain


def dot(a, b):
    return jnp.dot(a, b, preferred_element_type=F32)


def dot_t(a, b):
    return lax.dot_general(a, b, (((1,), (1,)), ((), ())), preferred_element_type=F32)


def tie(*values):
    return lax.optimization_barrier(values)


def ring(size):
    return [(i, (i + 1) % size) for i in range(size)], [(i, (i - 1) % size) for i in range(size)]


def x_swap(value):
    return lax.ppermute(value, "xh", SWAP)


class Beside:
    def __init__(self, values):
        self.values = list(values)
        self.results = []

    def start(self, moving):
        if len(self.results) < len(self.values):
            self.results.append(x_swap(tie(self.values[len(self.results)], moving)[0]))

    def end(self, *moving):
        if len(self.results) > 1:
            *moving, self.results[-2] = tie(*moving, self.results[-2])
        return moving


def ring_gather(block, axis, by_rows=True, values=()):
    size = lax.axis_size(axis)
    right, left = ring(size)
    here = lax.axis_index(axis)
    rows, columns = block.shape
    beside = Beside(values)
    out = jnp.zeros((size * rows, columns) if by_rows else (rows, size * columns), block.dtype)

    def put(out, part, owner, row):
        owner = lax.rem(owner + size, size)
        at = (owner * rows + row, 0) if by_rows else (row, owner * columns)
        return lax.dynamic_update_slice(out, part, at)

    out = put(out, block, here, 0)
    fwd = bwd = block
    for step in range(1, size // 2):
        beside.start(fwd)
        fwd = lax.ppermute(fwd, axis, right)
        bwd = lax.ppermute(bwd, axis, left)
        fwd, bwd = beside.end(fwd, bwd)
        out = put(out, fwd, here - step, 0)
        out = put(out, bwd, here + step, 0)
    half = rows // 2
    far = here - size // 2
    fwd = lax.ppermute(fwd[:half], axis, right)
    bwd = lax.ppermute(bwd[half:], axis, left)
    out = put(out, fwd, far, 0)
    return put(out, bwd, far, half), beside.results


def ring_scatter(partial, axis):
    size = lax.axis_size(axis)
    right, left = ring(size)
    here = lax.axis_index(axis)
    rows, half = partial.shape[0] // size, partial.shape[1] // 2

    def term(offset):
        return lax.dynamic_slice_in_dim(partial, lax.rem(here + offset + size, size) * rows, rows, 0)

    def add(a, b):
        return (a.astype(F32) + b.astype(F32)).astype(BF16)

    far = term(size // 2)
    fwd = lax.ppermute(far[:, :half], axis, right)
    bwd = lax.ppermute(far[:, half:], axis, left)
    for step in range(size // 2 - 1, 0, -1):
        ahead, behind = term(step), term(-step)
        if step == size // 2 - 1:
            fwd = jnp.concatenate([add(ahead[:, :half], fwd), ahead[:, half:]], axis=1)
            bwd = jnp.concatenate([behind[:, :half], add(behind[:, half:], bwd)], axis=1)
        else:
            fwd, bwd = add(ahead, fwd), add(behind, bwd)
        fwd = lax.ppermute(fwd, axis, right)
        bwd = lax.ppermute(bwd, axis, left)
    return term(0), fwd, bwd


def vmem_call(kernel, outs, name, limit, scratch=()):
    vmem = pl.BlockSpec(memory_space=pltpu.VMEM)

    def call(position, *args):
        return pl.pallas_call(
            kernel,
            out_shape=outs,
            in_specs=[pl.BlockSpec(memory_space=pltpu.SMEM)] + [vmem] * len(args),
            out_specs=jax.tree.map(lambda _: vmem, outs),
            scratch_shapes=scratch,
            compiler_params=pltpu.CompilerParams(vmem_limit_bytes=limit * MIB),
            name=name,
        )(position, *args)

    return call


def shape(rows, columns, dtype=BF16):
    return jax.ShapeDtypeStruct((rows, columns), dtype)


def attend(query, keys, values, seen):
    scores = jnp.where(seen, dot_t(query, keys) * SCALE, -1e30)
    probs = jnp.exp(scores - jnp.max(scores, axis=-1, keepdims=True))
    return probs, jnp.sum(probs, axis=-1, keepdims=True)


def spatial_kernel(place_ref, x_ref, gain_ref, own_ref, a_ref, b_ref, out_ref, h_ref):
    rows, model = x_ref.shape
    frame_q = (lax.broadcasted_iota(jnp.int32, (rows, rows), 0) // 8) % 2
    frame_k = (lax.broadcasted_iota(jnp.int32, (rows, rows), 1) // 8) % 2
    same = frame_q == frame_k
    core, position = place_ref[0], place_ref[1]
    half = model // 2
    first = pl.ds(pl.multiple_of(core * half, half), half)
    second = pl.ds(pl.multiple_of((1 - core) * half, half), half)

    norm_rows(x_ref, gain_ref, h_ref)

    def head(query, keys, values):
        probs, total = attend(query.astype(BF16), keys.astype(BF16), values.astype(BF16), same)
        return dot((probs / total).astype(BF16), values.astype(BF16)).astype(BF16)

    def split(kind):
        return dot(h_ref[:, first], a_ref[kind]) + dot(h_ref[:, second], b_ref[kind])

    hidden = h_ref[...]
    mine = head(*(dot(hidden, own_ref[kind]) for kind in range(3)))
    other = head(*(split(kind) for kind in range(3)))
    out_ref[:, :HEAD_DIM] = jnp.where(position == 0, mine, other)
    out_ref[:, HEAD_DIM:] = jnp.where(position == 0, other, mine)


def temporal_kernel(_, qkv_ref, out_ref):
    rows = qkv_ref.shape[0]
    times = qkv_ref[:, 6 * HEAD_DIM :].astype(F32)
    token_q = lax.broadcasted_iota(jnp.int32, (rows, rows), 0) % 8
    token_k = lax.broadcasted_iota(jnp.int32, (rows, rows), 1) % 8
    seen = (jnp.transpose(times)[:1] <= times[:, :1]) & (token_q == token_k)
    for head in range(2):
        query, keys, values = (
            qkv_ref[:, (2 * kind + head) * HEAD_DIM : (2 * kind + head + 1) * HEAD_DIM]
            for kind in range(3)
        )
        probs, total = attend(query, keys, values, seen)
        coarse = probs.astype(BF16)
        fine = (probs - coarse.astype(F32)).astype(BF16)
        result = (dot(coarse, values) + dot(fine, values)) / total
        out_ref[:, head * HEAD_DIM : (head + 1) * HEAD_DIM] = result.astype(BF16)


def out_step(heads_ref, w_ref, w2_ref, state_ref, all_ref):
    half, width = heads_ref.shape[1] // 2, state_ref.shape[1]
    total = dot(heads_ref[:, :half], w_ref[...].reshape(half, width))
    total += dot(heads_ref[:, half:], w2_ref[...].reshape(half, width))
    total += state_ref[...].astype(F32)
    step = pl.program_id(0)
    all_ref[:, pl.ds(pl.multiple_of(step * width, width), width)] = total
    return total


def norm_rows(all_ref, gain_ref, h_ref):
    @pl.loop(0, all_ref.shape[0] // 128)
    def _(tile):
        part = pl.ds(pl.multiple_of(tile * 128, 128), 128)
        h_ref[part] = normed(all_ref[part].astype(F32), gain_ref[...]).astype(BF16)


def project_kernel(place_ref, own_ref, q0, k0, v0, q1, k1, v1, _, out_ref, all_ref, h_ref):
    rows, model = h_ref.shape
    core, position = place_ref[0], place_ref[1]
    half = model // 2
    first = pl.ds(pl.multiple_of(core * half, half), half)
    second = pl.ds(pl.multiple_of((1 - core) * half, half), half)
    hidden = h_ref[...]
    for kind, (a, b) in enumerate(((q0, q1), (k0, k1), (v0, v1))):
        mine = dot(hidden, own_ref[kind]).astype(BF16)
        other = (dot(h_ref[:, first], a[...]) + dot(h_ref[:, second], b[...])).astype(BF16)
        start = 2 * kind * HEAD_DIM
        out_ref[:, start : start + HEAD_DIM] = jnp.where(position == 0, mine, other)
        out_ref[:, start + HEAD_DIM : start + 2 * HEAD_DIM] = jnp.where(position == 0, other, mine)
    frame = (lax.broadcasted_iota(jnp.int32, (rows, HEAD_DIM), 0) // 8) % 2
    times = jnp.where(frame == 0, place_ref[2], place_ref[3])
    out_ref[:, 6 * HEAD_DIM :] = times.astype(F32).astype(BF16)


def mlp_kernel(place_ref, in_ref, out_ref, *refs):
    *pieces, x_ref, o_ref, all_ref, h_ref = refs
    ins, outs = (pieces[:3], pieces[5:8]), (pieces[3:5], pieces[8:])
    own = x_ref.shape[0]
    x_ref[...] = all_ref[pl.ds(pl.multiple_of(place_ref[4] * own, own), own)]

    @pl.loop(0, h_ref.shape[0] // 256)
    def _(tile):
        rows = pl.ds(pl.multiple_of(tile * 256, 256), 256)

        def inner(weights):
            total, start = None, 0
            for w in weights:
                term = dot(h_ref[rows, start : start + w.shape[0]], w[...])
                total = term if total is None else total + term
                start += w.shape[0]
            return jax.nn.gelu(total, approximate=True).astype(BF16)

        units = jnp.concatenate([inner([in_ref]), inner(ins[0]), inner(ins[1])], axis=1)
        for block in range(o_ref.shape[1] // 256):
            columns = slice(block * 256, (block + 1) * 256)
            weight = [out_ref[:, columns]] + [w[:, columns] for w in (*outs[0], *outs[1])]
            o_ref[rows, columns] = dot(units, jnp.concatenate(weight, axis=0)).astype(BF16)


def out_call(kernel, name, outs, place, heads, weight, state, gain, *weights):
    rows, inputs = heads.shape
    blocks, width = 8, 256
    if weight.ndim == 3:
        halves = [pl.BlockSpec((1, inputs // 2, width), lambda c, i=i: (c, i, 0)) for i in range(2)]
    else:
        halves = [
            pl.BlockSpec((4, 1, width, width), lambda c, i=i: (i, c // 4, 0, c % 4)) for i in range(2)
        ]
    column = pl.BlockSpec((rows, width), lambda c: (0, c))
    count = len(weights)

    def once(value):
        return pl.BlockSpec(value.shape, lambda c: (0, 0), pipeline_mode=pl.Buffered(1))

    def whole(place_ref, heads_ref, w_ref, w2_ref, state_ref, gain_ref, *refs):
        sources, results = refs[:count], refs[count : count + 2]
        all_ref, h_ref, *held, sems = refs[count + 2 :]
        copies = [
            pltpu.make_async_copy(source, target, sems.at[i])
            for i, (source, target) in enumerate(zip(sources, held))
        ]

        @pl.when(pl.program_id(0) == 0)
        def _():
            for copy in copies:
                copy.start()

        total = out_step(heads_ref, w_ref, w2_ref, state_ref, all_ref)
        if outs[0][1]:
            results[0][...] = total

        @pl.when(pl.program_id(0) == blocks - 1)
        def _():
            norm_rows(all_ref, gain_ref, h_ref)
            for copy in copies:
                copy.wait()
            kernel(place_ref, *held, *results, all_ref, h_ref)

    return pl.pallas_call(
        whole,
        grid=(blocks,),
        out_shape=[out for out, _ in outs],
        in_specs=[
            pl.BlockSpec(memory_space=pltpu.SMEM),
            once(heads),
            *halves,
            column,
            once(gain),
        ]
        + [pl.BlockSpec(memory_space=pl.ANY)] * count,
        out_specs=[column if split else pl.BlockSpec(out.shape, lambda c: (0, 0)) for out, split in outs],
        scratch_shapes=[
            pltpu.VMEM((rows, blocks * width), F32),
            pltpu.VMEM((rows, blocks * width), BF16),
            *(pltpu.VMEM(value.shape, value.dtype) for value in weights),
            pltpu.SemaphoreType.DMA((count,)),
        ],
        compiler_params=pltpu.CompilerParams(vmem_limit_bytes=56 * MIB),
        name=name,
    )(place, heads, weight, weight, state, gain, *weights)


def body(
    video, frame_ids, gains, spatial_qkv, spatial_out, temporal_qkv, temporal_out, mlp_in, mlp_out
):
    xh, core = lax.axis_index("xh"), lax.axis_index("c")
    model = video.shape[-1]
    first = xh == 0
    times = lax.dynamic_slice_in_dim(frame_ids, 2 * xh, 2, 0)
    place = jnp.concatenate(
        [jnp.stack([core, xh]).astype(jnp.int32), times, lax.axis_index(Z).astype(jnp.int32)[None]]
    )

    def cut(value, index, parts, axis):
        size = value.shape[axis] // parts
        return lax.dynamic_slice_in_dim(value, index * size, size, axis)

    def core_swap(value):
        return lax.ppermute(value, "c", SWAP)

    grouped = jnp.transpose(video.reshape(2, 8, 4, model), (0, 2, 1, 3))
    got = x_swap(cut(grouped, 1 - xh, 2, 1))
    keep = cut(grouped, xh, 2, 1)
    state = jnp.concatenate(
        [jnp.where(first, keep, got), jnp.where(first, got, keep)], axis=0
    ).reshape(64, model)
    def paired(own, other):
        return jnp.concatenate([jnp.where(first, own, other), jnp.where(first, other, own)], axis=0)

    spatial_piece = cut(spatial_out, core, 2, 1)
    temporal_piece = cut(temporal_out, lax.axis_index("y") * 2 + core, 8, 1)
    other = x_swap(jnp.concatenate([spatial_piece, temporal_piece], axis=1))
    spatial_piece = paired(spatial_piece, other[:, : model // 2])
    temporal_piece = paired(temporal_piece, other[:, model // 2 :])
    state, spatial_piece = tie(state, spatial_piece)
    spatial_whole = lax.all_gather(spatial_piece, Z + ("c",), axis=0).reshape(8, 2, 256, model // 2)

    temporal_half = cut(temporal_qkv, core, 2, 1)
    in_half, out_half = cut(mlp_in, core, 2, 1), cut(mlp_out, core, 2, 0)

    state, (other,) = ring_gather(state, Z, True, [cut(spatial_qkv, core, 2, 1)])
    state, other = tie(state, other)
    in_a = x_swap(tie(in_half[:512], state)[0])
    heads = vmem_call(
        spatial_kernel, shape(512, 256), "spatial", 24, scratch=[pltpu.VMEM((512, model), BF16)]
    )(place, state, gains[:1], spatial_qkv, other, core_swap(other))
    heads, in_a = tie(heads, in_a)

    heads, others = ring_gather(heads, Z, False, [temporal_half[kind] for kind in range(3)])
    heads, *others = tie(heads, *others)
    others += [core_swap(other) for other in others]
    in_b = x_swap(tie(in_half[512:1536], heads)[0])
    temporal_piece = lax.all_gather(tie(temporal_piece, spatial_whole)[0], Z, axis=0, tiled=True)
    second, packed = out_call(
        project_kernel,
        "project",
        [(shape(512, model, F32), True), (shape(512, 7 * HEAD_DIM), False)],
        *(place, heads, spatial_whole, state, gains[1:2], temporal_qkv, *others),
    )
    packed, in_b = tie(packed, in_b)
    packed = lax.all_to_all(packed.reshape(32, 16, 7 * HEAD_DIM), PEERS, 0, 0, tiled=True)
    packed, temporal_piece = tie(packed, temporal_piece)
    temporal_whole = lax.all_gather(temporal_piece, ("y", "c"), axis=0)
    heads = vmem_call(temporal_kernel, shape(512, 2 * HEAD_DIM), "temporal", 20)(
        place, packed.reshape(512, 7 * HEAD_DIM)
    )
    heads = lax.all_to_all(heads.reshape(32, 16, 2 * HEAD_DIM), PEERS, 0, 0, tiled=True)
    heads, others = ring_gather(
        heads.reshape(512, 256), Z, False, [in_half[1536:], out_half[:128], out_half[128:]]
    )
    others = [in_a, in_b] + others
    third, partial = out_call(
        mlp_kernel,
        "mlp",
        [(shape(64, model, F32), False), (shape(512, model), False)],
        *(place, heads, temporal_whole, second, gains[2:3], mlp_in, mlp_out),
        *(others + [core_swap(other) for other in others]),
    )
    own, fwd, bwd = ring_scatter(partial, Z)
    result = third + (own.astype(F32) + fwd.astype(F32) + bwd.astype(F32))

    result = result.astype(BF16).reshape(2, 2, 2, 8, model)
    keep = lax.dynamic_index_in_dim(result, xh, 0, keepdims=False)
    got = x_swap(lax.dynamic_index_in_dim(result, 1 - xh, 0, keepdims=False))
    result = jnp.concatenate([jnp.where(first, keep, got), jnp.where(first, got, keep)], axis=1)
    return jnp.transpose(result, (0, 2, 1, 3)).reshape(16, 4, model)


def solution(mesh):
    fine = Mesh(mesh.devices.reshape(4, 2, 2, 4, 2, 2), TM + SPACE)
    return jax.shard_map(
        body,
        mesh=fine,
        in_specs=(
            P(SPACE, TM, None),
            P(TM),
            P(),
            P(None, None, SPACE),
            P(SPACE, None),
            P(None, None, SPACE),
            P(SPACE, None),
            P(None, SPACE),
            P(SPACE, None),
        ),
        out_specs=P(SPACE, TM, None),
        check_vma=False,
    )
```
